32 devices in a mesh: dp: 4 (over z), tile: 4 (over x, core), seq: 2 (over y).
Axes of the slice: x: 2, y: 2, z: 4, core: 2. Of those that a mesh axis runs over, the one named last changes fastest.
Arguments:
- features: bfloat16 [4, 8, 16, 32, 128], P('dp', None, 'tile'), may hold values from -6 to 6
- lengths: int32 [4], P('dp'), may hold values from 1 to 8, as said below
- weight: bfloat16 [3456, 5120], P(('dp', 'tile'), 'seq'), may hold values from -0.109375 to 0.109375
- bias: bfloat16 [5120], P('seq'), may hold values from -3 to 3
- cotangent: bfloat16 [4, 8, 16, 32, 5120], P('dp', 'seq', 'tile'), may hold values from -6 to 6
Outputs:
- pose_tokens: bfloat16 [4, 8, 16, 32, 5120], P('dp', 'seq', 'tile')
- grad_features: bfloat16 [4, 8, 16, 32, 128], P('dp', None, 'tile')
- grad_weight: float32 [3456, 5120], P(('dp', 'tile'), 'seq')
- grad_bias: float32 [5120], P('seq')
The draws below stay inside these ranges and needn't reach their ends.
Inputs may be any that keep to these rules, and one draw needn't show every extreme that they name: `lengths`: exactly one clip has 8 live frames; every other clip has at most 4.
All inputs are finite; a program needn't handle non-finite values.
Results may differ from the reference program's by a relative error of at most 0.005.
Values may be sent and summed in bfloat16 or wider, within the bound.
A program may use at most 512 MiB of HBM per device.

```python
import jax
import jax.numpy as jnp
from jax import lax

C = 128
D = 5120
FRAMES = 8
W = 32
CLIPS = 4
H = 16


def draw_lengths(key, part):
    mixed = jax.random.fold_in(key, 11)
    first_key, second_key = jax.random.split(mixed)
    others = jax.random.randint(first_key, (CLIPS,), 1, FRAMES // 2 + 1)
    longest = jax.random.randint(second_key, (), 0, CLIPS)
    return jnp.where(jnp.arange(CLIPS) == longest, FRAMES, others).astype(jnp.int32)


def shard_levels(key, dims, cuts, smallest, top_value):
    gain = 1.0
    for position, shards_of in cuts:
        steps = jax.random.uniform(jax.random.fold_in(jax.random.fold_in(key, 6), position), (shards_of,), jnp.float32, smallest / len(cuts), top_value / len(cuts))
        gain = gain * jnp.repeat(jnp.exp(steps), dims[position] // shards_of).reshape((-1,) + (1,) * (len(dims) - 1 - position))
    return gain


def bell_draw(rng, dims, spread, reach, cuts=(), dtype=jnp.bfloat16):
    result = jax.random.normal(rng, dims, jnp.float32) * spread
    if len(cuts) > 0:
        result = shard_levels(rng, dims, cuts, -0.22, 0.18) * result
    return jnp.clip(result, min=-reach, max=reach).astype(dtype)


def setup_inputs(seed: int = 0) -> dict:
    key_list = jax.random.split(jax.random.key(seed), 6)
    features = bell_draw(key_list[0], (CLIPS, FRAMES, H, W, C), 1.0, 6.0, ((0, 4), (2, 4)))
    lengths = draw_lengths(jax.random.fold_in(key_list[5], 71), 0)
    weight = bell_draw(key_list[2], (27 * C, D), (27 * C) ** -0.5, 0.109375, ((0, 16), (1, 2)))
    bias = bell_draw(key_list[3], (D,), 0.5, 3.0, ((0, 2),))
    cotangent = bell_draw(key_list[4], (CLIPS, FRAMES, H, W, D), 1.0, 6.0, ((0, 4), (1, 2), (2, 4)))
    return {"features": features, "lengths": lengths, "weight": weight, "bias": bias, "cotangent": cotangent}


def silu_grad(values):
    sigma = jax.nn.sigmoid(values)
    return sigma * (1.0 + values * (1.0 - sigma))

def reference(features, lengths, weight, bias, cotangent):
    kernel = weight.reshape(27, C, D)
    bias_f = bias.astype(jnp.float32)

    def per_clip(carry, item):
        clip_feat, clip_len, clip_cot = item
        frame_count, row_count, col_count = (clip_feat.shape[0], clip_feat.shape[1], clip_feat.shape[2])
        row_total = frame_count * row_count * col_count
        frame_mask = (jnp.arange(frame_count) < clip_len).astype(jnp.float32)[:, None, None, None]
        inner_vals = clip_feat.astype(jnp.float32)
        hidden = (jax.nn.silu(inner_vals) * frame_mask).astype(jnp.bfloat16)
        padded_feat = jnp.pad(hidden, ((1, 1), (1, 1), (1, 1), (0, 0)))
        grad_out = clip_cot * frame_mask.astype(jnp.bfloat16)
        padded_grad = jnp.pad(grad_out, ((1, 1), (1, 1), (1, 1), (0, 0)))
        flat_grad = grad_out.reshape(row_total, D)
        output = jnp.zeros((row_total, D), jnp.float32)
        grad_hidden = jnp.zeros((row_total, C), jnp.float32)
        pieces = []
        for tap_f in range(3):
            for tap_h in range(3):
                for tap_w in range(3):
                    index = (tap_f * 3 + tap_h) * 3 + tap_w
                    columns = padded_feat[tap_f:tap_f + frame_count, tap_h:tap_h + row_count, tap_w:tap_w + col_count].reshape(row_total, C)
                    output = output + jnp.dot(columns, kernel[index], preferred_element_type=jnp.float32)
                    pieces.append(jnp.dot(columns.T, flat_grad, preferred_element_type=jnp.float32))
                    behind = padded_grad[2 - tap_f:2 - tap_f + frame_count, 2 - tap_h:2 - tap_h + row_count, 2 - tap_w:2 - tap_w + col_count].reshape(row_total, D)
                    grad_hidden = grad_hidden + jnp.dot(behind, kernel[index].T, preferred_element_type=jnp.float32)
        tokens = ((output.reshape(frame_count, row_count, col_count, D) + bias_f) * frame_mask).astype(jnp.bfloat16)
        grad_feat = (silu_grad(inner_vals) * grad_hidden.reshape(frame_count, row_count, col_count, C) * frame_mask).astype(jnp.bfloat16)
        grad_w, grad_b = carry
        grad_w = grad_w + jnp.concatenate(pieces, 0)
        grad_b = grad_b + lax.optimization_barrier(jnp.sum(flat_grad.astype(jnp.float32), axis=0))
        return ((grad_w, grad_b), (tokens, grad_feat))
    start = (jnp.zeros((27 * C, D), jnp.float32), jnp.zeros((D,), jnp.float32))
    (grad_w, grad_b), (tokens, grad_feat) = lax.scan(per_clip, start, (features, lengths, cotangent))
    return (tokens, grad_feat, grad_w, grad_b)
```

```python
import jax
import jax.numpy as jnp
from jax import lax
from jax.sharding import PartitionSpec as P


def pick(pieces, index):
    result = pieces[0]
    for place in range(1, len(pieces)):
        result = jnp.where(index == place, pieces[place], result)
    return result


def swap(value, axis, distance):
    count = lax.axis_size(axis)
    return lax.ppermute(value, axis, [(i, i ^ distance) for i in range(count)])


def sum_over(value, axes):
    for axis in axes:
        distance = 1
        while distance < lax.axis_size(axis):
            value = value + swap(value, axis, distance)
            distance *= 2
    return value


def exchange(parts, axis):
    me = lax.axis_index(axis)
    count = lax.axis_size(axis)
    by_offset = [pick(parts, me)]
    for offset in range(1, count):
        by_offset.append(swap(pick(parts, me ^ offset), axis, offset))
    return [pick(by_offset, me ^ source) for source in range(count)]


def neighbours(low_row, high_row, axis):
    count = lax.axis_size(axis)
    forward = [(i, i + 1) for i in range(count - 1)]
    backward = [(i + 1, i) for i in range(count - 1)]
    return lax.ppermute(high_row, axis, forward), lax.ppermute(low_row, axis, backward)


def silu_grad(values):
    sigma = jax.nn.sigmoid(values)
    return sigma * (1.0 + values * (1.0 - sigma))


def shards(features, lengths, weight, bias, cotangent):
    seq_count = lax.axis_size("seq")
    local_feat = features[0]
    frame_count, row_count, col_count, chan_count = local_feat.shape
    row_total = frame_count * row_count * col_count
    share = weight.shape[1]
    frame_share = frame_count // seq_count
    frame_mask = (jnp.arange(frame_count) < lengths[0]).astype(jnp.float32)[:, None, None, None]

    cot = cotangent[0]
    received = exchange(
        [cot[..., j * share : (j + 1) * share] for j in range(seq_count)], "seq"
    )
    grad_out = jnp.concatenate(received, axis=0) * frame_mask.astype(jnp.bfloat16)
    flat_grad = grad_out.reshape(row_total, share)

    inner_vals = local_feat.astype(jnp.float32)
    hidden = (jax.nn.silu(inner_vals) * frame_mask).astype(jnp.bfloat16)
    above, below = neighbours(hidden[:, :1], hidden[:, -1:], "tile")
    padded = jnp.pad(
        jnp.concatenate([above, hidden, below], axis=1), ((1, 1), (0, 0), (1, 1), (0, 0))
    )
    wide = jnp.concatenate([padded[:, :, e : e + col_count] for e in range(3)], axis=3)
    columns = jnp.concatenate(
        [wide[a : a + frame_count, b : b + row_count] for a in range(3) for b in range(3)], axis=3
    ).reshape(row_total, 27 * chan_count)

    weight_term = lax.dot_general(
        columns, flat_grad, (((0,), (0,)), ((), ())), preferred_element_type=jnp.float32
    ).astype(jnp.bfloat16)
    grad_weight = lax.psum_scatter(
        weight_term, ("dp", "tile"), scatter_dimension=0, tiled=True
    ).astype(jnp.float32)
    grad_bias = sum_over(jnp.sum(flat_grad, axis=0, dtype=jnp.float32), ("tile", "dp"))

    full_weight = lax.all_gather(weight, ("dp", "tile"), axis=0, tiled=True)
    output = jnp.dot(columns, full_weight, preferred_element_type=jnp.float32)
    tokens = (
        (output.reshape(frame_count, row_count, col_count, share) + bias.astype(jnp.float32))
        * frame_mask
    ).astype(jnp.bfloat16)
    pose_tokens = jnp.concatenate(
        exchange(
            [tokens[j * frame_share : (j + 1) * frame_share] for j in range(seq_count)], "seq"
        ),
        axis=3,
    )

    spread = lax.dot_general(
        flat_grad, full_weight, (((1,), (1,)), ((), ())), preferred_element_type=jnp.float32
    ).reshape(frame_count, row_count, col_count, 27 * chan_count)
    total = jnp.zeros((frame_count, row_count + 2, col_count, chan_count), jnp.float32)
    for a in range(3):
        for b in range(3):
            start = (a * 3 + b) * 3 * chan_count
            first = spread[..., start : start + chan_count]
            second = spread[..., start + chan_count : start + 2 * chan_count]
            third = spread[..., start + 2 * chan_count : start + 3 * chan_count]
            none = ((0, 0), (0, 0))
            joined = (
                jnp.pad(first[:, :, 1:], (*none, (0, 1), (0, 0)))
                + second
                + jnp.pad(third[:, :, :-1], (*none, (1, 0), (0, 0)))
            )
            kept = joined[max(0, 1 - a) : frame_count - max(0, a - 1)]
            total = total + jnp.pad(
                kept, ((max(0, a - 1), max(0, 1 - a)), (b, 2 - b), (0, 0), (0, 0))
            )
    from_above, from_below = neighbours(total[:, :1], total[:, -1:], "tile")
    rims = jnp.concatenate(
        [from_above, jnp.zeros_like(total[:, 2:-2]), from_below], axis=1
    )
    grad_hidden = sum_over(total[:, 1:-1] + rims, ("seq",))
    grad_features = (silu_grad(inner_vals) * grad_hidden * frame_mask).astype(jnp.bfloat16)
    return (pose_tokens[None], grad_features[None], grad_weight, grad_bias)


def solution(mesh):
    return jax.shard_map(
        shards,
        mesh=mesh,
        in_specs=(
            P("dp", None, "tile", None, None),
            P("dp"),
            P(("dp", "tile"), "seq"),
            P("seq"),
            P("dp", "seq", "tile", None, None),
        ),
        out_specs=(
            P("dp", "seq", "tile", None, None),
            P("dp", None, "tile", None, None),
            P(("dp", "tile"), "seq"),
            P("seq"),
        ),
        check_vma=False,
    )
```

```python
import jax
import jax.numpy as jnp
from jax import lax
from jax.sharding import PartitionSpec as P


def pick(pieces, index):
    result = pieces[0]
    for place in range(1, len(pieces)):
        result = jnp.where(index == place, pieces[place], result)
    return result


def swap(value, axis, distance):
    count = lax.axis_size(axis)
    return lax.ppermute(value, axis, [(i, i ^ distance) for i in range(count)])


def sum_over(value, axes):
    for axis in axes:
        distance = 1
        while distance < lax.axis_size(axis):
            value = value + swap(value, axis, distance)
            distance *= 2
    return value


def exchange(parts, axis):
    me = lax.axis_index(axis)
    count = lax.axis_size(axis)
    by_offset = [pick(parts, me)]
    for offset in range(1, count):
        by_offset.append(swap(pick(parts, me ^ offset), axis, offset))
    return [pick(by_offset, me ^ source) for source in range(count)]


def neighbours(low_row, high_row, axis):
    count = lax.axis_size(axis)
    forward = [(i, i + 1) for i in range(count - 1)]
    backward = [(i + 1, i) for i in range(count - 1)]
    return lax.ppermute(high_row, axis, forward), lax.ppermute(low_row, axis, backward)


def scatter(value, dim, axis, index, count, stride):
    total = lax.dynamic_index_in_dim(value, index, dim, keepdims=False)
    for offset in range(1, count):
        leaving = lax.dynamic_index_in_dim(value, index ^ offset, dim, keepdims=False)
        arrived = swap(leaving.astype(jnp.bfloat16), axis, offset * stride)
        total = total + arrived.astype(jnp.float32)
    return total


def scatter_rows(value, start, width, tile_first):
    dp, tile = lax.axis_index("dp"), lax.axis_index("tile")
    dp_count, pair_count = lax.axis_size("dp"), lax.axis_size("tile") // 2
    value = value.reshape(dp_count, pair_count, 2, -1, value.shape[1])
    sizes = (dp_count, pair_count, 1, value.shape[3], width)

    def rows_of(parity):
        return lax.dynamic_slice(value, (0, 0, parity, 0, start), sizes)[:, :, 0]

    arrived = swap(rows_of((tile & 1) ^ 1).astype(jnp.bfloat16), "tile", 1)
    value = rows_of(tile & 1) + arrived.astype(jnp.float32)
    if tile_first:
        value = scatter(value, 1, "tile", tile >> 1, pair_count, 2)
        return scatter(value, 0, "dp", dp, dp_count, 1)
    value = scatter(value, 0, "dp", dp, dp_count, 1)
    return scatter(value, 0, "tile", tile >> 1, pair_count, 2)


def silu_grad(values):
    sigma = jax.nn.sigmoid(values)
    return sigma * (1.0 + values * (1.0 - sigma))


def shards(features, lengths, weight, bias, cotangent):
    seq_count = lax.axis_size("seq")
    local_feat = features[0]
    frame_count, row_count, col_count, chan_count = local_feat.shape
    row_total = frame_count * row_count * col_count
    share = weight.shape[1]
    frame_share = frame_count // seq_count
    frame_mask = (jnp.arange(frame_count) < lengths[0]).astype(jnp.float32)[:, None, None, None]

    cot = cotangent[0]
    received = exchange(
        [cot[..., j * share : (j + 1) * share] for j in range(seq_count)], "seq"
    )
    grad_out = jnp.concatenate(received, axis=0) * frame_mask.astype(jnp.bfloat16)
    flat_grad = grad_out.reshape(row_total, share)

    inner_vals = local_feat.astype(jnp.float32)
    hidden = (jax.nn.silu(inner_vals) * frame_mask).astype(jnp.bfloat16)
    above, below = neighbours(hidden[:, :1], hidden[:, -1:], "tile")
    padded = jnp.pad(
        jnp.concatenate([above, hidden, below], axis=1), ((1, 1), (0, 0), (1, 1), (0, 0))
    )
    wide = jnp.concatenate([padded[:, :, e : e + col_count] for e in range(3)], axis=3)
    columns = jnp.concatenate(
        [wide[a : a + frame_count, b : b + row_count] for a in range(3) for b in range(3)], axis=3
    ).reshape(row_total, 27 * chan_count)

    weight_term = lax.dot_general(
        columns, flat_grad, (((0,), (0,)), ((), ())), preferred_element_type=jnp.float32
    )
    half = share // 2
    grad_weight = jnp.concatenate(
        [
            scatter_rows(weight_term, 0, half, True),
            scatter_rows(weight_term, half, share - half, False),
        ],
        axis=1,
    )
    grad_bias = sum_over(jnp.sum(flat_grad, axis=0, dtype=jnp.float32), ("tile", "dp"))

    full_weight = lax.all_gather(weight, ("dp", "tile"), axis=0, tiled=True)
    bias_vals = bias.astype(jnp.float32) + 0.0 * weight_term[0, 0]
    output = jnp.dot(columns, full_weight, preferred_element_type=jnp.float32)
    tokens = (
        (output.reshape(frame_count, row_count, col_count, share) + bias_vals)
        * frame_mask
    ).astype(jnp.bfloat16)
    pose_tokens = jnp.concatenate(
        exchange(
            [tokens[j * frame_share : (j + 1) * frame_share] for j in range(seq_count)], "seq"
        ),
        axis=3,
    )

    after = 0.0 * tokens[0, 0, 0, 0].astype(jnp.float32)
    spread = lax.dot_general(
        flat_grad, full_weight, (((1,), (1,)), ((), ())), preferred_element_type=jnp.float32
    )
    spread = (spread + after).reshape(frame_count, row_count, col_count, 27 * chan_count)
    total = jnp.zeros((frame_count, row_count + 2, col_count, chan_count), jnp.float32)
    for a in range(3):
        for b in range(3):
            start = (a * 3 + b) * 3 * chan_count
            first = spread[..., start : start + chan_count]
            second = spread[..., start + chan_count : start + 2 * chan_count]
            third = spread[..., start + 2 * chan_count : start + 3 * chan_count]
            none = ((0, 0), (0, 0))
            joined = (
                jnp.pad(first[:, :, 1:], (*none, (0, 1), (0, 0)))
                + second
                + jnp.pad(third[:, :, :-1], (*none, (1, 0), (0, 0)))
            )
            kept = joined[max(0, 1 - a) : frame_count - max(0, a - 1)]
            total = total + jnp.pad(
                kept, ((max(0, a - 1), max(0, 1 - a)), (b, 2 - b), (0, 0), (0, 0))
            )
    from_above, from_below = neighbours(total[:, :1], total[:, -1:], "tile")
    rims = jnp.concatenate(
        [from_above, jnp.zeros_like(total[:, 2:-2]), from_below], axis=1
    )
    grad_hidden = sum_over(total[:, 1:-1] + rims, ("seq",))
    grad_features = (silu_grad(inner_vals) * grad_hidden * frame_mask).astype(jnp.bfloat16)
    return (pose_tokens[None], grad_features[None], grad_weight, grad_bias)


def solution(mesh):
    return jax.shard_map(
        shards,
        mesh=mesh,
        in_specs=(
            P("dp", None, "tile", None, None),
            P("dp"),
            P(("dp", "tile"), "seq"),
            P("seq"),
            P("dp", "seq", "tile", None, None),
        ),
        out_specs=(
            P("dp", "seq", "tile", None, None),
            P("dp", None, "tile", None, None),
            P(("dp", "tile"), "seq"),
            P("seq"),
        ),
        check_vma=False,
    )
```

```python
import jax
import jax.numpy as jnp
from jax import lax
from jax.sharding import PartitionSpec as P


def pick(pieces, index):
    result = pieces[0]
    for place in range(1, len(pieces)):
        result = jnp.where(index == place, pieces[place], result)
    return result


def swap(value, axis, distance):
    count = lax.axis_size(axis)
    return lax.ppermute(value, axis, [(i, i ^ distance) for i in range(count)])


def sum_over(value, axes):
    for axis in axes:
        distance = 1
        while distance < lax.axis_size(axis):
            value = value + swap(value, axis, distance)
            distance *= 2
    return value


def exchange(parts, axis):
    me = lax.axis_index(axis)
    count = lax.axis_size(axis)
    by_offset = [pick(parts, me)]
    for offset in range(1, count):
        by_offset.append(swap(pick(parts, me ^ offset), axis, offset))
    return [pick(by_offset, me ^ source) for source in range(count)]


def neighbours(low_row, high_row, axis):
    count = lax.axis_size(axis)
    forward = [(i, i + 1) for i in range(count - 1)]
    backward = [(i + 1, i) for i in range(count - 1)]
    return lax.ppermute(high_row, axis, forward), lax.ppermute(low_row, axis, backward)


def scatter_start(value, dim, axis, index, count, stride):
    terms = [lax.dynamic_index_in_dim(value, index, dim, keepdims=False)]
    for offset in range(1, count):
        leaving = lax.dynamic_index_in_dim(value, index ^ offset, dim, keepdims=False)
        terms.append(swap(leaving.astype(jnp.bfloat16), axis, offset * stride))
    return terms


def scatter_end(terms, after):
    total = terms[0] + after
    for term in terms[1:]:
        total = total + term.astype(jnp.float32)
    return total


def pair_rows(value, start, width):
    tile = lax.axis_index("tile")
    dp_count, pair_count = lax.axis_size("dp"), lax.axis_size("tile") // 2
    value = value.reshape(dp_count, pair_count, 2, -1, value.shape[1])
    sizes = (dp_count, pair_count, 1, value.shape[3], width)

    def rows_of(parity):
        return lax.dynamic_slice(value, (0, 0, parity, 0, start), sizes)[:, :, 0]

    arrived = swap(rows_of((tile & 1) ^ 1).astype(jnp.bfloat16), "tile", 1)
    return rows_of(tile & 1) + arrived.astype(jnp.float32)


def scatter_tile(value):
    tile = lax.axis_index("tile")
    return scatter_start(value, value.ndim - 3, "tile", tile >> 1, lax.axis_size("tile") // 2, 2)


def scatter_dp(value):
    return scatter_start(value, 0, "dp", lax.axis_index("dp"), lax.axis_size("dp"), 1)


def silu_grad(values):
    sigma = jax.nn.sigmoid(values)
    return sigma * (1.0 + values * (1.0 - sigma))


def shards(features, lengths, weight, bias, cotangent):
    seq_count = lax.axis_size("seq")
    local_feat = features[0]
    frame_count, row_count, col_count, chan_count = local_feat.shape
    row_total = frame_count * row_count * col_count
    share = weight.shape[1]
    frame_share = frame_count // seq_count
    frame_mask = (jnp.arange(frame_count) < lengths[0]).astype(jnp.float32)[:, None, None, None]

    cot = cotangent[0]
    received = exchange(
        [cot[..., j * share : (j + 1) * share] for j in range(seq_count)], "seq"
    )
    grad_out = jnp.concatenate(received, axis=0) * frame_mask.astype(jnp.bfloat16)
    flat_grad = grad_out.reshape(row_total, share)

    inner_vals = local_feat.astype(jnp.float32)
    hidden = (jax.nn.silu(inner_vals) * frame_mask).astype(jnp.bfloat16)
    above, below = neighbours(hidden[:, :1], hidden[:, -1:], "tile")
    padded = jnp.pad(
        jnp.concatenate([above, hidden, below], axis=1), ((1, 1), (0, 0), (1, 1), (0, 0))
    )
    wide = jnp.concatenate([padded[:, :, e : e + col_count] for e in range(3)], axis=3)
    columns = jnp.concatenate(
        [wide[a : a + frame_count, b : b + row_count] for a in range(3) for b in range(3)], axis=3
    ).reshape(row_total, 27 * chan_count)

    weight_term = lax.dot_general(
        columns, flat_grad, (((0,), (0,)), ((), ())), preferred_element_type=jnp.float32
    )
    units = share // 128
    last = max(1, units * 3 // 10)
    first = (units - last) // 2
    widths = [128 * first, 128 * (units - last - first), 128 * last]
    starts = [0, widths[0], widths[0] + widths[1]]
    partials = [pair_rows(weight_term, c, w) for c, w in zip(starts, widths)]
    moving = [scatter_tile(partials[0]), scatter_dp(partials[2]), scatter_tile(partials[1])]
    grad_bias = lax.psum(jnp.sum(flat_grad, axis=0, dtype=jnp.float32), ("dp", "tile"))

    full_weight = lax.all_gather(weight, ("dp", "tile"), axis=0, tiled=True)
    bias_vals = bias.astype(jnp.float32) + 0.0 * weight_term[0, 0]
    output = jnp.dot(columns, full_weight, preferred_element_type=jnp.float32)
    tokens = (
        (output.reshape(frame_count, row_count, col_count, share) + bias_vals)
        * frame_mask
    ).astype(jnp.bfloat16)
    pose_tokens = jnp.concatenate(
        exchange(
            [tokens[j * frame_share : (j + 1) * frame_share] for j in range(seq_count)], "seq"
        ),
        axis=3,
    )

    after = 0.0 * tokens[0, 0, 0, 0].astype(jnp.float32)
    spread = lax.dot_general(
        flat_grad, full_weight, (((1,), (1,)), ((), ())), preferred_element_type=jnp.float32
    )
    moving = [
        scatter_dp(scatter_end(moving[0], after)),
        scatter_tile(scatter_end(moving[1], after)),
        scatter_dp(scatter_end(moving[2], after)),
    ]
    spread = (spread + after).reshape(frame_count, row_count, col_count, 27 * chan_count)
    late = 0.0 * spread[0, 0, 0, 0]
    ended = [scatter_end(terms, late) for terms in moving]
    grad_weight = jnp.concatenate([ended[0], ended[2], ended[1]], axis=1)
    total = jnp.zeros((frame_count, row_count + 2, col_count, chan_count), jnp.float32)
    for a in range(3):
        for b in range(3):
            start = (a * 3 + b) * 3 * chan_count
            first = spread[..., start : start + chan_count]
            second = spread[..., start + chan_count : start + 2 * chan_count]
            third = spread[..., start + 2 * chan_count : start + 3 * chan_count]
            none = ((0, 0), (0, 0))
            joined = (
                jnp.pad(first[:, :, 1:], (*none, (0, 1), (0, 0)))
                + second
                + jnp.pad(third[:, :, :-1], (*none, (1, 0), (0, 0)))
            )
            kept = joined[max(0, 1 - a) : frame_count - max(0, a - 1)]
            total = total + jnp.pad(
                kept, ((max(0, a - 1), max(0, 1 - a)), (b, 2 - b), (0, 0), (0, 0))
            )
    from_above, from_below = neighbours(total[:, :1], total[:, -1:], "tile")
    rims = jnp.concatenate(
        [from_above, jnp.zeros_like(total[:, 2:-2]), from_below], axis=1
    )
    grad_hidden = sum_over(total[:, 1:-1] + rims, ("seq",))
    grad_features = (silu_grad(inner_vals) * grad_hidden * frame_mask).astype(jnp.bfloat16)
    return (pose_tokens[None], grad_features[None], grad_weight, grad_bias)


def solution(mesh):
    return jax.shard_map(
        shards,
        mesh=mesh,
        in_specs=(
            P("dp", None, "tile", None, None),
            P("dp"),
            P(("dp", "tile"), "seq"),
            P("seq"),
            P("dp", "seq", "tile", None, None),
        ),
        out_specs=(
            P("dp", "seq", "tile", None, None),
            P("dp", None, "tile", None, None),
            P(("dp", "tile"), "seq"),
            P("seq"),
        ),
        check_vma=False,
    )
```

```python
import jax
import jax.numpy as jnp
from jax import lax
from jax.sharding import PartitionSpec as P


def pick(pieces, index):
    result = pieces[0]
    for place in range(1, len(pieces)):
        result = jnp.where(index == place, pieces[place], result)
    return result


def swap(value, axis, distance):
    count = lax.axis_size(axis)
    return lax.ppermute(value, axis, [(i, i ^ distance) for i in range(count)])


def sum_over(value, axes):
    for axis in axes:
        distance = 1
        while distance < lax.axis_size(axis):
            value = value + swap(value, axis, distance)
            distance *= 2
    return value


def exchange(parts, axis):
    me = lax.axis_index(axis)
    count = lax.axis_size(axis)
    by_offset = [pick(parts, me)]
    for offset in range(1, count):
        by_offset.append(swap(pick(parts, me ^ offset), axis, offset))
    return [pick(by_offset, me ^ source) for source in range(count)]


def neighbours(low_row, high_row, axis):
    count = lax.axis_size(axis)
    forward = [(i, i + 1) for i in range(count - 1)]
    backward = [(i + 1, i) for i in range(count - 1)]
    return lax.ppermute(high_row, axis, forward), lax.ppermute(low_row, axis, backward)


def scatter_start(value, dim, axis, index, count, stride):
    terms = [lax.dynamic_index_in_dim(value, index, dim, keepdims=False)]
    for offset in range(1, count):
        leaving = lax.dynamic_index_in_dim(value, index ^ offset, dim, keepdims=False)
        terms.append(swap(leaving.astype(jnp.bfloat16), axis, offset * stride))
    return terms


def scatter_end(terms, after):
    total = terms[0] + after
    for term in terms[1:]:
        total = total + term.astype(jnp.float32)
    return total


def pair_rows(value, start, width):
    tile = lax.axis_index("tile")
    dp_count, pair_count = lax.axis_size("dp"), lax.axis_size("tile") // 2
    value = value.reshape(dp_count, pair_count, 2, -1, value.shape[1])
    sizes = (dp_count, pair_count, 1, value.shape[3], width)

    def rows_of(parity):
        return lax.dynamic_slice(value, (0, 0, parity, 0, start), sizes)[:, :, 0]

    arrived = swap(rows_of((tile & 1) ^ 1).astype(jnp.bfloat16), "tile", 1)
    return rows_of(tile & 1) + arrived.astype(jnp.float32)


def scatter_tile(value):
    tile = lax.axis_index("tile")
    return scatter_start(value, value.ndim - 3, "tile", tile >> 1, lax.axis_size("tile") // 2, 2)


def scatter_dp(value):
    return scatter_start(value, 0, "dp", lax.axis_index("dp"), lax.axis_size("dp"), 1)


def silu_grad(values):
    sigma = jax.nn.sigmoid(values)
    return sigma * (1.0 + values * (1.0 - sigma))


def shards(features, lengths, weight, bias, cotangent):
    seq_count = lax.axis_size("seq")
    local_feat = features[0]
    frame_count, row_count, col_count, chan_count = local_feat.shape
    row_total = frame_count * row_count * col_count
    share = weight.shape[1]
    frame_share = frame_count // seq_count
    frame_mask = (jnp.arange(frame_count) < lengths[0]).astype(jnp.float32)[:, None, None, None]

    cot = cotangent[0]
    received = exchange(
        [cot[..., j * share : (j + 1) * share] for j in range(seq_count)], "seq"
    )
    grad_out = jnp.concatenate(received, axis=0) * frame_mask.astype(jnp.bfloat16)
    flat_grad = grad_out.reshape(row_total, share)

    inner_vals = local_feat.astype(jnp.float32)
    hidden = (jax.nn.silu(inner_vals) * frame_mask).astype(jnp.bfloat16)
    above, below = neighbours(hidden[:, :1], hidden[:, -1:], "tile")
    padded = jnp.pad(
        jnp.concatenate([above, hidden, below], axis=1), ((1, 1), (0, 0), (1, 1), (0, 0))
    )
    wide = jnp.concatenate([padded[:, :, e : e + col_count] for e in range(3)], axis=3)
    columns = jnp.concatenate(
        [wide[a : a + frame_count, b : b + row_count] for a in range(3) for b in range(3)], axis=3
    ).reshape(row_total, 27 * chan_count)

    weight_term = lax.dot_general(
        columns, flat_grad, (((0,), (0,)), ((), ())), preferred_element_type=jnp.float32
    )
    units = share // 128
    last = max(1, units * 3 // 10)
    first = (units - last) // 2
    widths = [128 * first, 128 * (units - last - first), 128 * last]
    starts = [0, widths[0], widths[0] + widths[1]]
    grad_bias = sum_over(jnp.sum(flat_grad, axis=0, dtype=jnp.float32), ("dp", "tile"))
    settled = 0.0 * grad_bias[0]
    partials = [pair_rows(weight_term, c, w) + settled for c, w in zip(starts, widths)]
    moving = [scatter_tile(partials[0]), scatter_dp(partials[2])]
    full_weight = lax.all_gather(weight, ("dp", "tile"), axis=0, tiled=True)
    bias_vals = bias.astype(jnp.float32) + 0.0 * weight_term[0, 0]
    output = jnp.dot(columns, full_weight, preferred_element_type=jnp.float32)
    tokens = (
        (output.reshape(frame_count, row_count, col_count, share) + bias_vals)
        * frame_mask
    ).astype(jnp.bfloat16)
    pose_tokens = jnp.concatenate(
        exchange(
            [tokens[j * frame_share : (j + 1) * frame_share] for j in range(seq_count)], "seq"
        ),
        axis=3,
    )

    after = 0.0 * tokens[0, 0, 0, 0].astype(jnp.float32)
    added = scatter_end(moving[0], after)
    then = 0.0 * added[0, 0, 0]
    moving = [scatter_dp(added), moving[1], scatter_tile(partials[1] + after)]
    spread = lax.dot_general(
        flat_grad, full_weight, (((1,), (1,)), ((), ())), preferred_element_type=jnp.float32
    )
    spread = (spread + then).reshape(frame_count, row_count, col_count, 27 * chan_count)
    late = 0.0 * spread[0, 0, 0, 0]
    moving = [
        moving[0],
        scatter_tile(scatter_end(moving[1], then)),
        scatter_dp(scatter_end(moving[2], then)),
    ]
    ended = [scatter_end(terms, late) for terms in moving]
    grad_weight = jnp.concatenate([ended[0], ended[2], ended[1]], axis=1)
    total = jnp.zeros((frame_count, row_count + 2, col_count, chan_count), jnp.float32)
    for a in range(3):
        for b in range(3):
            start = (a * 3 + b) * 3 * chan_count
            first = spread[..., start : start + chan_count]
            second = spread[..., start + chan_count : start + 2 * chan_count]
            third = spread[..., start + 2 * chan_count : start + 3 * chan_count]
            none = ((0, 0), (0, 0))
            joined = (
                jnp.pad(first[:, :, 1:], (*none, (0, 1), (0, 0)))
                + second
                + jnp.pad(third[:, :, :-1], (*none, (1, 0), (0, 0)))
            )
            kept = joined[max(0, 1 - a) : frame_count - max(0, a - 1)]
            total = total + jnp.pad(
                kept, ((max(0, a - 1), max(0, 1 - a)), (b, 2 - b), (0, 0), (0, 0))
            )
    from_above, from_below = neighbours(total[:, :1], total[:, -1:], "tile")
    rims = jnp.concatenate(
        [from_above, jnp.zeros_like(total[:, 2:-2]), from_below], axis=1
    )
    grad_hidden = sum_over(total[:, 1:-1] + rims, ("seq",))
    grad_features = (silu_grad(inner_vals) * grad_hidden * frame_mask).astype(jnp.bfloat16)
    return (pose_tokens[None], grad_features[None], grad_weight, grad_bias)


def solution(mesh):
    return jax.shard_map(
        shards,
        mesh=mesh,
        in_specs=(
            P("dp", None, "tile", None, None),
            P("dp"),
            P(("dp", "tile"), "seq"),
            P("seq"),
            P("dp", "seq", "tile", None, None),
        ),
        out_specs=(
            P("dp", "seq", "tile", None, None),
            P("dp", None, "tile", None, None),
            P(("dp", "tile"), "seq"),
            P("seq"),
        ),
        check_vma=False,
    )
```
